512 devices in a mesh: pipe: 8 (over z), seq: 64 (over x, y, core).
Axes of the slice: x: 4, y: 8, z: 8, core: 2. Of those that a mesh axis runs over, the one named last changes fastest.
Arguments:
- activations: bfloat16 [8, 8192, 2048], P('pipe', 'seq'), may hold values from -6 to 6
- norm_gain: float32 [8, 2048], P('pipe'), may hold values from 0.1 to 1.9
- conv_kernels: float32 [8, 3, 4, 2048], P('pipe'), may hold values from -3 to 3
- out_gain: float32 [8, 2048], P('pipe'), may hold values from 0.1 to 1.9
Outputs:
- handed: bfloat16 [8, 8192, 2048], P('pipe', 'seq')
The draws below stay inside these ranges and needn't reach their ends.
All inputs are finite; a program needn't handle non-finite values.
Results may differ from the reference program's by a relative error of at most 0.0052.
Values may be sent and summed in bfloat16 or wider, within the bound.
A program may use at most 192 MiB of HBM per device.

```python
import jax
import jax.numpy as jnp
from jax import lax

DH = 128
KW = 4
TOK_DEV = 128
C = 2048
SECTIONS = 8
TOKENS = 8192


def steps_of(key, shape, cuts, low, largest):
    factor_of, own = 1.0, jax.random.fold_in(key, 6)
    for axis_at, parts in cuts:
        heights = jnp.exp(jax.random.uniform(jax.random.fold_in(own, axis_at), (parts,), jnp.float32, low / len(cuts), largest / len(cuts)))
        factor_of = factor_of * jnp.repeat(heights, shape[axis_at] // parts).reshape([-1 if axis == axis_at else 1 for axis in range(len(shape))])
    return factor_of


def bell_draw(key, dims, deviation, most, cuts=(), kind=jnp.bfloat16):
    drawn = jax.random.normal(key, dims, jnp.float32) * deviation
    if len(cuts) > 0:
        drawn = steps_of(key, dims, cuts, -0.22, 0.18) * drawn
    return jnp.clip(drawn, min=-most, max=most).astype(kind)


def setup_inputs(seed: int = 0) -> dict:
    key_of = jax.random.split(jax.random.key(seed), 5)
    activations = bell_draw(key_of[0], (SECTIONS, TOKENS, C), 1.0, 6.0, ((0, 8), (1, 64)))
    norm_gain = jnp.clip(1.0 + 0.18 * jax.random.normal(key_of[1], (SECTIONS, C), jnp.float32), 0.1, 1.9)
    conv_kernels = bell_draw(key_of[2], (SECTIONS, 3, KW, C), KW ** -0.5, 3.0, ((0, 8),), jnp.float32)
    out_gain = jnp.clip(1.0 + 0.18 * jax.random.normal(key_of[3], (SECTIONS, C), jnp.float32), 0.1, 1.9)
    return {"activations": activations, "norm_gain": norm_gain, "conv_kernels": conv_kernels, "out_gain": out_gain}


def normalize(row_block, row_gain):
    row_values = row_block.astype(jnp.float32)
    factor = lax.rsqrt(lax.optimization_barrier(jnp.mean(row_values * row_values, axis=-1, keepdims=True)) + 1e-06)
    return (row_values * factor * row_gain).astype(jnp.bfloat16)

def convolve(padded, kernel, kernel_width, tok_count):
    summed = jnp.zeros((tok_count, padded.shape[1]), jnp.float32)
    for offset in range(kernel_width):
        first_row = kernel_width - 1 - offset
        summed = summed + kernel[offset] * padded[first_row:first_row + tok_count].astype(jnp.float32)
    return summed

def run_section(section_rows, gain_in, kernels, gain_out):
    kernel_width = kernels.shape[1]
    tok_count = section_rows.shape[0]
    channels = section_rows.shape[1]
    head_count = channels // DH
    normed = normalize(section_rows, gain_in)
    padded = jnp.concatenate([jnp.zeros((kernel_width - 1, channels), jnp.bfloat16), normed], 0)
    query_all = (jax.nn.elu(convolve(padded, kernels[0], kernel_width, tok_count)) + 1.0).astype(jnp.bfloat16)
    key_all = (jax.nn.elu(convolve(padded, kernels[1], kernel_width, tok_count)) + 1.0).astype(jnp.bfloat16)
    value_all = convolve(padded, kernels[2], kernel_width, tok_count).astype(jnp.bfloat16)
    blocks = tok_count // TOK_DEV

    def split_blocks(matrix):
        return matrix.reshape(blocks, TOK_DEV, head_count, DH).transpose(0, 2, 1, 3)
    causal = jnp.tril(jnp.ones((TOK_DEV, TOK_DEV), dtype=bool))
    highest = lax.Precision.HIGHEST

    def advance(prefix, pieces):
        query_h, key_h, value_h = pieces
        query_f = query_h.astype(jnp.float32)
        key_f = key_h.astype(jnp.float32)
        value_f = value_h.astype(jnp.float32)
        carried = jnp.einsum('htd,hde->hte', query_f, prefix, precision=highest)
        scores = jnp.einsum('htd,hud->htu', query_f, key_f, precision=highest)
        weights = jnp.where(causal, scores, 0.0).astype(jnp.bfloat16)
        weights = lax.optimization_barrier(weights).astype(jnp.float32)
        within = jnp.einsum('htu,hue->hte', weights, value_f, precision=highest)
        mixed_out = carried + within
        own = jnp.einsum('htd,hte->hde', key_f, value_f, precision=highest)
        return (prefix + own, mixed_out)
    zero_state = jnp.zeros((head_count, DH, DH), jnp.float32)
    unused, mixed_out = lax.scan(advance, zero_state, (split_blocks(query_all), split_blocks(key_all), split_blocks(value_all)))
    scaled = mixed_out * lax.rsqrt(lax.optimization_barrier(jnp.mean(mixed_out * mixed_out, axis=-1, keepdims=True)) + 1e-06)
    merged = scaled.transpose(0, 2, 1, 3).reshape(tok_count, channels)
    return (section_rows.astype(jnp.float32) + merged * gain_out).astype(jnp.bfloat16)

def reference(activations, norm_gain, conv_kernels, out_gain):
    results = []
    for section in range(SECTIONS):
        results.append(run_section(activations[section], norm_gain[section], conv_kernels[section], out_gain[section]))
    stacked = jnp.stack(results, 0)
    return jnp.roll(stacked, 1, axis=0)
```

```python
import functools

import jax
import jax.numpy as jnp
from jax import lax
from jax.experimental import pallas as pl
from jax.experimental.pallas import tpu as pltpu
from jax.sharding import PartitionSpec as P

DH = 128
HALO = 16
MESH = pl.DeviceIdType.MESH
F32 = jnp.float32
BF16 = jnp.bfloat16


def lanes(start, size):
    return pl.ds(pl.multiple_of(start, DH), size)


def kernel(
    n_pipe, n_chip, tok, heads,
    act, ngain, conv, ogain, out,
    own, xbuf, fbuf, pconv, pngain, pogain, halo, hsend, nbuf,
    qbuf, kbuf, vbuf, within, tsend, trecv, psend, pbuf, rbuf,
    load_sem, xs_sem, xr_sem, fs_sem, fr_sem, ps_sem, pr_sem, hs_sem, hr_sem,
    ts_sem, tr_sem, qs_sem, qr_sem, rs_sem, rr_sem,
):
    wide = heads * DH
    rows = 2 * tok
    part = wide // n_chip
    width = 4 * wide
    pipe = lax.axis_index("pipe")
    seq = lax.axis_index("seq")
    core = seq % 2
    chip = seq // 2
    ahead = (pipe + 1) % n_pipe
    behind = (pipe + n_pipe - 1) % n_pipe
    peer = seq + 1 - 2 * core

    def a_cols(which):
        return which * (2 * wide)

    def b_cols(which):
        return which * (2 * wide) + wide

    def local(src, dst, sem):
        return pltpu.make_async_copy(src, dst, sem)

    def remote(src, dst, send, recv, to_pipe, to_seq):
        return pltpu.make_async_remote_copy(
            src_ref=src, dst_ref=dst, send_sem=send, recv_sem=recv,
            device_id=(to_pipe, to_seq), device_id_type=MESH,
        )

    barrier = pltpu.get_barrier_semaphore()

    def greet(step, carry):
        other = 2 * ((chip + step) % n_chip) + core
        pl.semaphore_signal(barrier, inc=1, device_id=(pipe, other), device_id_type=MESH)
        return carry

    pl.semaphore_signal(barrier, inc=1, device_id=(pipe, peer), device_id_type=MESH)
    for which in range(2):
        pl.semaphore_signal(
            barrier, inc=1, device_id=(behind, 2 * chip + which), device_id_type=MESH
        )
    lax.fori_loop(1, n_chip, greet, 0)

    loads = [
        local(act, own, load_sem.at[0]),
        local(act.at[:, lanes(a_cols(core), wide)], xbuf.at[0, core], load_sem.at[1]),
        local(conv.at[:, :, lanes(a_cols(core), wide)], pconv.at[0], load_sem.at[2]),
        local(ngain.at[:, lanes(a_cols(core), wide)], pngain.at[0], load_sem.at[3]),
        local(ogain.at[:, lanes(a_cols(core), wide)], pogain.at[0], load_sem.at[4]),
    ]
    for load in loads:
        load.start()
    pl.semaphore_wait(barrier, n_chip + 2)

    x_copies = [
        remote(
            act.at[:, lanes(a_cols(1 - core), wide)], xbuf.at[0, core],
            xs_sem.at[0], xr_sem.at[0], pipe, peer,
        )
    ]
    for which in range(2):
        x_copies.append(
            remote(
                act.at[:, lanes(b_cols(which), wide)], xbuf.at[1, core],
                xs_sem.at[1 + which], xr_sem.at[1 + core], ahead, 2 * chip + which,
            )
        )
    p_copies = [
        remote(
            conv.at[:, :, lanes(b_cols(core), wide)], pconv.at[1],
            ps_sem.at[0], pr_sem.at[0], ahead, seq,
        ),
        remote(
            ngain.at[:, lanes(b_cols(core), wide)], pngain.at[1],
            ps_sem.at[1], pr_sem.at[1], ahead, seq,
        ),
        remote(
            ogain.at[:, lanes(b_cols(core), wide)], pogain.at[1],
            ps_sem.at[2], pr_sem.at[2], ahead, seq,
        ),
    ]
    for copy in x_copies + p_copies:
        copy.start()

    loads[0].wait()
    squares = jnp.zeros((tok, DH), F32)
    for piece in range(width // DH):
        values = own[:, piece * DH : (piece + 1) * DH].astype(F32)
        squares = squares + values * values
    mean = jnp.sum(squares, axis=-1, keepdims=True) * (1.0 / width)
    factor = jnp.broadcast_to(lax.rsqrt(mean + 1e-06), (tok, DH))
    fbuf[0, core] = factor.T[:8]
    f_copies = [
        remote(
            fbuf.at[0, core], fbuf.at[0, core], fs_sem.at[0], fr_sem.at[0], pipe, peer
        )
    ]
    for which in range(2):
        f_copies.append(
            remote(
                fbuf.at[0, core], fbuf.at[1, core],
                fs_sem.at[1 + which], fr_sem.at[1 + core], ahead, 2 * chip + which,
            )
        )
    for copy in f_copies:
        copy.start()

    def normalize(group):
        for block in range(2):
            column = jnp.broadcast_to(fbuf[group, block, 0:1, :], (tok, tok)).T

            def one(head, carry):
                cols = lanes(head * DH, DH)
                normed = (
                    xbuf[group, block, :, cols].astype(F32) * column * pngain[group, :, cols]
                ).astype(BF16)
                nbuf[group, pl.ds(HALO + block * tok, tok), cols] = normed.astype(F32)
                if block == 1:
                    hsend[group, :, cols] = normed[tok - HALO :]
                return carry

            lax.fori_loop(0, heads, one, 0)

    def h_copy(group):
        return remote(
            hsend.at[group], halo.at[group], hs_sem.at[group], hr_sem.at[group],
            pipe, 2 * ((chip + 1) % n_chip) + core,
        )

    def convolve(group, head, start, count):
        cols = lanes(head * DH, DH)
        shifted = [nbuf[group, pl.ds(HALO + start - i, count), cols] for i in range(4)]
        made = []
        for j in range(3):
            total = pconv[group, j, 0:1, cols] * shifted[0]
            for i in range(1, 4):
                total = total + pconv[group, j, i : i + 1, cols] * shifted[i]
            made.append(total)

        def positive(x):
            return jnp.where(x > 0.0, x + 1.0, jnp.exp(jnp.minimum(x, 0.0)))

        where = pl.ds(start, count)
        qbuf[group, where, cols] = positive(made[0]).astype(BF16)
        kbuf[group, where, cols] = positive(made[1]).astype(BF16)
        vbuf[group, where, cols] = made[2].astype(BF16)

    tile = tok // 2

    def to_states(group):
        normalize(group)
        h_copy(group).start()

        def later_rows(head, carry):
            for start in range(tile, rows, tile):
                convolve(group, head, start, tile)
            return carry

        lax.fori_loop(0, heads, later_rows, 0)
        h_copy(group).wait_recv()
        first = jnp.where(chip == 0, 0.0, halo[group].astype(F32))
        nbuf[group, 0:HALO, :] = first

        def first_rows(head, carry):
            cols = lanes(head * DH, DH)
            convolve(group, head, 0, tile)
            state = lax.dot_general(
                kbuf[group, :, cols], vbuf[group, :, cols], (((0,), (0,)), ((), ())),
                preferred_element_type=F32,
            )
            tsend[group, lanes(head * DH, DH), :] = state.astype(BF16)
            return carry

        lax.fori_loop(0, heads, first_rows, 0)

        def one(step, carry):
            other = (chip + step) % n_chip
            remote(
                tsend.at[group, pl.ds(pl.multiple_of(other * part, part), part)],
                trecv.at[group, chip], ts_sem.at[group], tr_sem.at[group],
                pipe, 2 * other + core,
            ).start()
            return carry

        lax.fori_loop(1, n_chip, one, 0)
        trecv[group, chip] = tsend[group, pl.ds(pl.multiple_of(chip * part, part), part), :]

    def inside(group):
        causal = lax.broadcasted_iota(jnp.int32, (rows, rows), 1) <= lax.broadcasted_iota(
            jnp.int32, (rows, rows), 0
        )

        def one(head, carry):
            cols = lanes(head * DH, DH)
            scores = lax.dot_general(
                qbuf[group, :, cols], kbuf[group, :, cols], (((1,), (1,)), ((), ())),
                preferred_element_type=F32,
            )
            weights = jnp.where(causal, scores, 0.0).astype(BF16)
            within[group, :, cols] = jnp.dot(
                weights, vbuf[group, :, cols], preferred_element_type=F32
            )
            return carry

        lax.fori_loop(0, heads, one, 0)

    def t_wait(group):
        return remote(
            psend.at[group, pl.ds(0, n_chip - 1)], trecv.at[group, pl.ds(0, n_chip - 1)],
            ts_sem.at[group], tr_sem.at[group], pipe, peer,
        )

    def q_wait(group):
        count = (n_chip - 1) * part
        return remote(
            tsend.at[group, pl.ds(0, count)], pbuf.at[group, pl.ds(0, count)],
            qs_sem.at[group], qr_sem.at[group], pipe, peer,
        )

    def prefixes(group):
        t_wait(group).wait_recv()

        def add(index, total):
            psend[group, index] = total.astype(BF16)
            return total + trecv[group, index].astype(F32)

        lax.fori_loop(0, n_chip, add, jnp.zeros((part, DH), F32))

        def one(step, carry):
            other = (chip + step) % n_chip
            remote(
                psend.at[group, other],
                pbuf.at[group, pl.ds(pl.multiple_of(chip * part, part), part)],
                qs_sem.at[group], qr_sem.at[group], pipe, 2 * other + core,
            ).start()
            return carry

        lax.fori_loop(1, n_chip, one, 0)
        pbuf[group, pl.ds(pl.multiple_of(chip * part, part), part), :] = psend[group, chip]

    def finish(group, send):
        q_wait(group).wait_recv()

        def one(head, carry):
            cols = lanes(head * DH, DH)
            mixed = within[group, :, cols] + jnp.dot(
                qbuf[group, :, cols], pbuf[group, lanes(head * DH, DH), :],
                preferred_element_type=F32,
            )
            scaled = mixed * lax.rsqrt(
                jnp.mean(mixed * mixed, axis=-1, keepdims=True) + 1e-06
            ) * pogain[group, :, cols]
            for block in range(2):
                residual = xbuf[group, block, :, cols].astype(F32)
                rbuf[group, block, :, cols] = (
                    residual + scaled[block * tok : (block + 1) * tok]
                ).astype(BF16)
            if send is not None:
                send(head)
            return carry

        lax.fori_loop(0, heads, one, 0)

    def hand(head):
        for block in range(2):
            remote(
                rbuf.at[0, block, :, lanes(head * DH, DH)],
                out.at[:, lanes(a_cols(core) + head * DH, DH)],
                rs_sem.at[block], rr_sem.at[core], ahead, 2 * chip + block,
            ).start()

    for load in loads[1:]:
        load.wait()
    x_copies[0].wait_recv()
    f_copies[0].wait_recv()
    to_states(0)
    inside(0)
    prefixes(0)

    for which in range(2):
        remote(
            xbuf.at[0, 0], xbuf.at[1, which], xs_sem.at[0], xr_sem.at[1 + which], ahead, seq
        ).wait_recv()
        remote(
            fbuf.at[0, 0], fbuf.at[1, which], fs_sem.at[0], fr_sem.at[1 + which], ahead, seq
        ).wait_recv()
    for copy in p_copies:
        copy.wait_recv()
    to_states(1)
    finish(0, hand)
    inside(1)
    prefixes(1)
    finish(1, None)
    keep = local(
        rbuf.at[1, core], out.at[:, lanes(b_cols(core), wide)], load_sem.at[0]
    )
    give = remote(
        rbuf.at[1, 1 - core], out.at[:, lanes(b_cols(core), wide)],
        rs_sem.at[2], rr_sem.at[2], pipe, peer,
    )
    keep.start()
    give.start()

    for copy in x_copies + p_copies + f_copies:
        copy.wait_send()
    for group in range(2):
        h_copy(group).wait_send()
        t_wait(group).wait_send()
        q_wait(group).wait_send()
    for which in range(2):
        handed = remote(
            rbuf.at[0, which], out.at[:, lanes(a_cols(which), wide)],
            rs_sem.at[which], rr_sem.at[which], ahead, seq,
        )
        handed.wait_send()
        handed.wait_recv()
    keep.wait()
    give.wait_send()
    give.wait_recv()


def body(activations, norm_gain, conv_kernels, out_gain):
    n_pipe = lax.axis_size("pipe")
    n_chip = lax.axis_size("seq") // 2
    _, tok, width = activations.shape
    wide = width // 4
    heads = wide // DH
    part = wide // n_chip
    rows = 2 * tok
    dma = pltpu.SemaphoreType.DMA
    handed = pl.pallas_call(
        functools.partial(kernel, n_pipe, n_chip, tok, heads),
        out_shape=jax.ShapeDtypeStruct((tok, width), BF16),
        in_specs=[pl.BlockSpec(memory_space=pl.ANY)] * 4,
        out_specs=pl.BlockSpec(memory_space=pl.ANY),
        scratch_shapes=[
            pltpu.VMEM((tok, width), BF16),
            pltpu.VMEM((2, 2, tok, wide), BF16),
            pltpu.VMEM((2, 2, 8, tok), F32),
            pltpu.VMEM((2, 3, 4, wide), F32),
            pltpu.VMEM((2, 1, wide), F32),
            pltpu.VMEM((2, 1, wide), F32),
            pltpu.VMEM((2, HALO, wide), BF16),
            pltpu.VMEM((2, HALO, wide), BF16),
            pltpu.VMEM((2, HALO + rows, wide), F32),
            pltpu.VMEM((2, rows, wide), BF16),
            pltpu.VMEM((2, rows, wide), BF16),
            pltpu.VMEM((2, rows, wide), BF16),
            pltpu.VMEM((2, rows, wide), F32),
            pltpu.VMEM((2, wide, DH), BF16),
            pltpu.VMEM((2, n_chip, part, DH), BF16),
            pltpu.VMEM((2, n_chip, part, DH), BF16),
            pltpu.VMEM((2, wide, DH), BF16),
            pltpu.VMEM((2, 2, tok, wide), BF16),
            dma((5,)), dma((3,)), dma((3,)), dma((3,)), dma((3,)), dma((3,)), dma((3,)),
            dma((2,)), dma((2,)), dma((2,)), dma((2,)), dma((2,)), dma((2,)), dma((3,)), dma((3,)),
        ],
        compiler_params=pltpu.CompilerParams(
            collective_id=0, has_side_effects=True, vmem_limit_bytes=40 * 1024 * 1024
        ),
    )(activations[0], norm_gain, conv_kernels[0], out_gain)
    return handed[None]


def solution(mesh):
    placed = (P("pipe", "seq", None), P("pipe", None), P("pipe", None, None, None), P("pipe", None))
    return jax.shard_map(
        body, mesh=mesh, in_specs=placed, out_specs=P("pipe", "seq", None), check_vma=False
    )
```

```python
import functools

import jax
import jax.numpy as jnp
from jax import lax
from jax.experimental import pallas as pl
from jax.experimental.pallas import tpu as pltpu
from jax.sharding import PartitionSpec as P

DH = 128
HALO = 16
GROUPS = 2
PIECES = 4
OWNER = (0, 0)
EARLY = 2
ROW = 8
MESH = pl.DeviceIdType.MESH
F32 = jnp.float32
BF16 = jnp.bfloat16


def lanes(start, size):
    return pl.ds(pl.multiple_of(start, DH), size)


def kernel(
    n_pipe, n_chip, n_y, tok, heads,
    act, ngain, conv, ogain, out,
    own, sx, sf, column, pconv, pngain, pogain, snb, sk, sv, hsend, chalo, rhalo,
    tsend, trecv, rsend, rrecv, psend, pbuf, rx, rf, rnb, rq, rk, rv, within, res,
    load_sem, xs, xr, fs, fr, ps, pr, hs, hr, gs, gr, zs, zr,
    ts, tr, es, er, qs, qr, os_sem, or_sem,
):
    wide = heads * DH
    rows = 2 * tok
    each = heads // GROUPS
    gwide = each * DH
    part = gwide // n_y
    n_x = n_chip // n_y
    pipe = lax.axis_index("pipe")
    seq = lax.axis_index("seq")
    core = seq % 2
    chip = seq // 2
    x_at = chip // n_y
    y_at = chip % n_y
    ahead = (pipe + 1) % n_pipe
    behind = (pipe + n_pipe - 1) % n_pipe
    peer = seq + 1 - 2 * core
    next_chip = (chip + 1) % n_chip
    last_chip = (chip + n_chip - 1) % n_chip
    y_steps = sorted(range(1, n_y), key=lambda k: -min(k, n_y - k))
    x_steps = sorted(range(1, n_x), key=lambda k: -min(k, n_x - k))

    def on_row(step):
        return (y_at + step) % n_y

    def row_seq(y):
        return 2 * (x_at * n_y + y) + core

    def column_seq(x):
        return 2 * (x * n_y + y_at) + core

    def remote(src, dst, send, recv, to_pipe, to_seq):
        return pltpu.make_async_remote_copy(
            src_ref=src, dst_ref=dst, send_sem=send, recv_sem=recv,
            device_id=(to_pipe, to_seq), device_id_type=MESH,
        )

    def greet(to_pipe, to_seq):
        pl.semaphore_signal(barrier, inc=1, device_id=(to_pipe, to_seq), device_id_type=MESH)

    pending = []

    def finished():
        for wait in pending:
            wait()

    barrier = pltpu.get_barrier_semaphore()
    greet(pipe, peer)
    for which in range(2):
        greet(behind, 2 * chip + which)
    greet(pipe, 2 * last_chip + 1)
    for step in y_steps:
        greet(pipe, row_seq(on_row(step)))
        if 1 in OWNER:
            greet(behind, row_seq(on_row(step)))
    for step in x_steps:
        greet(pipe, column_seq((x_at + step) % n_x))

    half = lanes(core * wide, wide)
    loads = [
        pltpu.make_async_copy(act, own, load_sem.at[0]),
        pltpu.make_async_copy(conv.at[:, :, half], pconv.at[0], load_sem.at[1]),
        pltpu.make_async_copy(ngain, pngain.at[0], load_sem.at[2]),
    ]
    for load in loads:
        load.start()
    for load in loads:
        load.wait()

    squares = jnp.zeros((tok, DH), F32)
    for piece in range(2 * wide // DH):
        values = own[:, piece * DH : (piece + 1) * DH].astype(F32)
        squares = squares + values * values
    mean = jnp.sum(squares, axis=-1, keepdims=True) * (1.0 / (2 * wide))
    factor = jnp.broadcast_to(lax.rsqrt(mean + 1e-06), (tok, DH))
    column[0] = factor
    sf[0] = factor.T[:8]

    def halo_rows(head, carry):
        cols = lanes(head * DH, DH)
        hsend[:, cols] = (
            own[tok - HALO :, cols].astype(F32) * column[0, tok - HALO :, :] * pngain[0, :, cols]
        ).astype(BF16)
        return carry

    lax.fori_loop(0, 2 * heads, halo_rows, 0)

    def positive(x):
        return jnp.where(x > 0.0, x + 1.0, jnp.exp(jnp.minimum(x, 0.0)))

    def convolved(ref, start, count, which, j, cols):
        total = pconv[which, j, 0:1, cols] * ref[pl.ds(HALO + start, count), cols]
        for i in range(1, 4):
            total = total + pconv[which, j, i : i + 1, cols] * ref[
                pl.ds(HALO + start - i, count), cols
            ]
        return total

    def keys_values(slot, start, count, head):
        cols = lanes(head * DH, DH)
        ref = snb.at[slot]
        where = pl.ds(slot * tok + start, count)
        sk[where, cols] = positive(convolved(ref, start, count, 0, 1, cols)).astype(BF16)
        sv[where, cols] = convolved(ref, start, count, 0, 2, cols).astype(BF16)

    def state_rows(slot, first, last):
        def one(head, carry):
            cols = lanes(head * DH, DH)
            raw = own[:, lanes(core * wide + head * DH, DH)] if slot == 0 else sx[:, cols]
            normed = (
                raw.astype(F32) * column[slot] * pngain[0, :, lanes(core * wide + head * DH, DH)]
            ).astype(BF16)
            snb[slot, HALO:, cols] = normed.astype(F32)
            keys_values(slot, HALO, tok - HALO, head)
            return carry

        lax.fori_loop(first, last, one, 0, unroll=True)

    state_rows(0, 0, heads)

    pl.semaphore_wait(barrier, 3 + (1 + (1 in OWNER)) * len(y_steps) + len(x_steps) + 2 * core)
    x_copies = [
        remote(
            act.at[:, lanes((1 - core) * wide + group * gwide, gwide)],
            sx.at[:, pl.ds(group * gwide, gwide)],
            xs.at[group], xr.at[group], pipe, peer,
        )
        for group in range(GROUPS)
    ]
    f_copies = [remote(sf.at[0], sf.at[1], fs.at[0], fr.at[0], pipe, peer)]
    for which in range(2):
        f_copies.append(
            remote(sf.at[0], rf.at[core], fs.at[1 + which], fr.at[1 + core], ahead, 2 * chip + which)
        )
    h_copies = [
        remote(
            hsend.at[:, pl.ds(which * wide, wide)], chalo,
            hs.at[which], hr, pipe, 2 * next_chip + which,
        )
        for which in range(2)
    ]
    p_copies = [
        remote(conv.at[:, :, half], pconv.at[1], ps.at[0], pr.at[0], ahead, seq),
        remote(ngain, pngain.at[1], ps.at[1], pr.at[1], ahead, seq),
        remote(ogain, pogain, ps.at[2], pr.at[2], ahead, seq),
    ]

    pwide = wide // PIECES

    def raw_copy(piece, which):
        return remote(
            act.at[:, pl.ds(which * wide + piece * pwide, pwide)],
            rx.at[core, :, pl.ds(piece * pwide, pwide)],
            zs.at[piece, which], zr.at[piece, core], ahead, 2 * chip + which,
        )

    def send_raw(first, last):
        for piece in range(first, last):
            for which in range(2):
                copy = raw_copy(piece, which)
                copy.start()
                pending.append(copy.wait_send)

    @pl.when(core == 1)
    def _():
        for copy in h_copies:
            copy.start()

    f_copies[0].start()
    for copy in x_copies:
        copy.start()
    for copy in f_copies[1:] + p_copies:
        copy.start()
    send_raw(0, EARLY)

    def wait_sent_halo():
        @pl.when(core == 1)
        def _():
            for copy in h_copies:
                copy.wait_send()

    pending.append(wait_sent_halo)
    pending.extend(copy.wait_send for copy in x_copies)
    pending.append(f_copies[0].wait_send)
    pending.extend(copy.wait_send for copy in f_copies[1:] + p_copies)

    f_copies[0].wait_recv()
    column[1] = jnp.broadcast_to(sf[1, 0:1, :], (tok, tok)).T
    g_copy = remote(chalo, rhalo, gs, gr, ahead, seq)

    def edges(group):
        cols = pl.ds(group * gwide, gwide)
        before = jnp.where(chip == 0, 0.0, chalo[:, cols].astype(F32))
        snb[0, :HALO, cols] = jnp.where(core == 0, before, snb[1, tok:, cols])
        snb[1, :HALO, cols] = jnp.where(core == 0, snb[0, tok:, cols], before)

    def t_copy(group, y):
        return remote(
            tsend.at[group, pl.ds(pl.multiple_of(y * part, part), part)],
            trecv.at[group, y_at], ts.at[group], tr.at[group],
            (pipe, ahead)[OWNER[group]], row_seq(y),
        )

    def t_all(group):
        count = n_y - 1 + OWNER[group]
        return remote(
            psend.at[group, pl.ds(0, count)], trecv.at[group, pl.ds(0, count)],
            ts.at[group], tr.at[group], pipe, peer,
        )

    def slice_of(y):
        return pl.ds(pl.multiple_of(y * part, part), part)

    for group in range(GROUPS):
        x_copies[group].wait_recv()
        state_rows(1, group * each, (group + 1) * each)
    h_copies[0].wait_recv()
    g_copy.start()
    pending.append(g_copy.wait_send)
    for group in range(GROUPS):
        edges(group)

        def one(index, carry, group=group):
            head = group * each + index
            cols = lanes(head * DH, DH)
            for slot in range(2):
                keys_values(slot, 0, HALO, head)
            state = lax.dot_general(
                sk[:, cols], sv[:, cols], (((0,), (0,)), ((), ())), preferred_element_type=F32
            )
            tsend[group, lanes(index * DH, DH), :] = state.astype(BF16)
            return carry

        lax.fori_loop(0, each, one, 0, unroll=True)
        for step in y_steps + [0] * OWNER[group]:
            t_copy(group, on_row(step)).start()
        if OWNER[group] == 0:
            trecv[group, y_at] = tsend[group, slice_of(y_at), :]
        pending.append(t_all(group).wait_send)
    send_raw(EARLY, PIECES)

    def arrived_raw(piece):
        for which in range(2):
            remote(
                sx.at[:, pl.ds(0, pwide)], rx.at[which, :, pl.ds(piece * pwide, pwide)],
                xs.at[0], zr.at[piece, which], ahead, seq,
            ).wait_recv()

    def arrived_first():
        for which in range(2):
            remote(sf.at[0], rf.at[which], fs.at[0], fr.at[1 + which], ahead, seq).wait_recv()
        for copy in p_copies:
            copy.wait_recv()
        g_copy.wait_recv()

    def e_copy(group, x):
        return remote(
            rsend.at[group], rrecv.at[group, x_at], es.at[group], er.at[group], pipe, column_seq(x)
        )

    def e_all(group):
        return remote(
            psend.at[group, pl.ds(0, n_x - 1)], rrecv.at[group, pl.ds(0, n_x - 1)],
            es.at[group], er.at[group], pipe, peer,
        )

    def q_copy(group, y):
        return remote(
            psend.at[group, y], pbuf.at[group, slice_of(y_at)],
            qs.at[group], qr.at[group], (ahead, pipe)[OWNER[group]], row_seq(y),
        )

    def q_all(group):
        count = (n_y - OWNER[group]) * part
        return remote(
            tsend.at[group, pl.ds(0, count)], pbuf.at[group, pl.ds(0, count)],
            qs.at[group], qr.at[group], ahead, seq,
        )

    def totals(group):
        t_all(group).wait_recv()
        total = trecv[group, 0].astype(F32)
        for y in range(1, n_y):
            total = total + trecv[group, y].astype(F32)
        rsend[group] = total.astype(BF16)
        for step in x_steps:
            e_copy(group, (x_at + step) % n_x).start()
        rrecv[group, x_at] = rsend[group]
        pending.append(e_all(group).wait_send)

    def prefixes(group):
        e_all(group).wait_recv()
        total = jnp.zeros((part, DH), F32)
        for x in range(n_x):
            total = total + jnp.where(x < x_at, rrecv[group, x].astype(F32), 0.0)
        for y in range(n_y):
            psend[group, y] = total.astype(BF16)
            total = total + trecv[group, y].astype(F32)
        for step in y_steps + [0] * (1 - OWNER[group]):
            q_copy(group, on_row(step)).start()
        if OWNER[group] == 1:
            pbuf[group, slice_of(y_at), :] = psend[group, y_at]
        pending.append(q_all(group).wait_send)

    def own_half(head):
        return lanes(core * wide + head * DH, DH)

    def first_of_behind():
        arrived_first()
        for block in range(2):
            column[block] = jnp.broadcast_to(rf[block, 0:1, :], (tok, tok)).T
        rnb[:HALO, :] = jnp.where(chip == 0, 0.0, rhalo[...].astype(F32))

    def inside(piece):
        arrived_raw(piece)
        tile = tok // 2
        query_at = lax.broadcasted_iota(jnp.int32, (tok, rows), 0)
        key_at = lax.broadcasted_iota(jnp.int32, (tok, rows), 1)

        def one(index, carry):
            head = piece * (heads // PIECES) + index
            cols = lanes(head * DH, DH)
            for block in range(2):
                normed = (
                    rx[block, :, cols].astype(F32) * column[block] * pngain[1, :, own_half(head)]
                ).astype(BF16)
                rnb[pl.ds(HALO + block * tok, tok), cols] = normed.astype(F32)
            for start in range(0, rows, tile):
                where = pl.ds(start, tile)
                rq[where, cols] = positive(convolved(rnb, start, tile, 1, 0, cols)).astype(BF16)
                rk[where, cols] = positive(convolved(rnb, start, tile, 1, 1, cols)).astype(BF16)
                rv[where, cols] = convolved(rnb, start, tile, 1, 2, cols).astype(BF16)
            for block in range(2):
                here, until = pl.ds(block * tok, tok), (block + 1) * tok
                scores = lax.dot_general(
                    rq[here, cols], rk[:until, cols], (((1,), (1,)), ((), ())),
                    preferred_element_type=F32,
                )
                causal = key_at[:, :until] <= query_at[:, :until] + block * tok
                weights = jnp.where(causal, scores, 0.0).astype(BF16)
                within[here, cols] = jnp.dot(
                    weights, rv[:until, cols], preferred_element_type=F32
                )
            return carry

        lax.fori_loop(0, heads // PIECES, one, 0, unroll=True)

    def o_copy(head):
        return remote(
            res.at[1 - core, :, lanes(head * DH, DH)], out.at[:, own_half(head)],
            os_sem.at[0], or_sem, pipe, peer,
        )

    def keep_copy(head):
        return pltpu.make_async_copy(
            res.at[core, :, lanes(head * DH, DH)], out.at[:, own_half(head)], os_sem.at[1]
        )

    def finish(group):
        q_all(group).wait_recv()

        def one(index, carry):
            head = group * each + index
            cols = lanes(head * DH, DH)
            mixed = within[:, cols] + jnp.dot(
                rq[:, cols], pbuf[group, lanes(index * DH, DH), :], preferred_element_type=F32
            )
            square = jnp.dot(
                (mixed * mixed).astype(BF16), jnp.full((DH, DH), 1.0 / DH, BF16),
                preferred_element_type=F32,
            )
            scaled = mixed * lax.rsqrt(square + 1e-06) * pogain[:, own_half(head)]
            for block in range(2):
                res[block, :, cols] = (
                    rx[block, :, cols].astype(F32) + scaled[block * tok : (block + 1) * tok]
                ).astype(BF16)
            o_copy(head).start()
            keep_copy(head).start()
            return carry

        lax.fori_loop(0, each, one, 0, unroll=True)

    totals(0)
    if OWNER[1] == 0:
        totals(1)
    prefixes(0)
    if OWNER[1] == 0:
        prefixes(1)
    first_of_behind()
    for piece in range(PIECES // 2):
        inside(piece)
    if OWNER[1] == 1:
        totals(1)
        prefixes(1)
    for piece in range(PIECES // 2, PIECES):
        inside(piece)
    for group in range(GROUPS):
        finish(group)

    everything = remote(
        res.at[1 - core], out.at[:, lanes((1 - core) * wide, wide)], os_sem.at[0], or_sem, pipe, peer
    )
    everything.wait_send()
    everything.wait_recv()
    pltpu.make_async_copy(res.at[core], out.at[:, half], os_sem.at[1]).wait()
    finished()


def body(activations, norm_gain, conv_kernels, out_gain):
    n_pipe = lax.axis_size("pipe")
    n_chip = lax.axis_size("seq") // 2
    n_y = min(ROW, n_chip)
    n_x = n_chip // n_y
    _, tok, width = activations.shape
    wide = width // 2
    heads = wide // DH
    gwide = wide // GROUPS
    part = gwide // n_y
    rows = 2 * tok
    dma = pltpu.SemaphoreType.DMA
    handed = pl.pallas_call(
        functools.partial(kernel, n_pipe, n_chip, n_y, tok, heads),
        out_shape=jax.ShapeDtypeStruct((tok, width), BF16),
        in_specs=[pl.BlockSpec(memory_space=pltpu.HBM)] * 4,
        out_specs=pl.BlockSpec(memory_space=pl.ANY),
        scratch_shapes=[
            pltpu.VMEM((tok, width), BF16),
            pltpu.VMEM((tok, wide), BF16),
            pltpu.VMEM((2, 8, tok), F32),
            pltpu.VMEM((2, tok, DH), F32),
            pltpu.VMEM((2, 3, 4, wide), F32),
            pltpu.VMEM((2, 1, width), F32),
            pltpu.VMEM((1, width), F32),
            pltpu.VMEM((2, HALO + tok, wide), F32),
            pltpu.VMEM((rows, wide), BF16),
            pltpu.VMEM((rows, wide), BF16),
            pltpu.VMEM((HALO, width), BF16),
            pltpu.VMEM((HALO, wide), BF16),
            pltpu.VMEM((HALO, wide), BF16),
            pltpu.VMEM((GROUPS, gwide, DH), BF16),
            pltpu.VMEM((GROUPS, n_y, part, DH), BF16),
            pltpu.VMEM((GROUPS, part, DH), BF16),
            pltpu.VMEM((GROUPS, n_x, part, DH), BF16),
            pltpu.VMEM((GROUPS, n_y, part, DH), BF16),
            pltpu.VMEM((GROUPS, gwide, DH), BF16),
            pltpu.VMEM((2, tok, wide), BF16),
            pltpu.VMEM((2, 8, tok), F32),
            pltpu.VMEM((HALO + rows, wide), F32),
            pltpu.VMEM((rows, wide), BF16),
            pltpu.VMEM((rows, wide), BF16),
            pltpu.VMEM((rows, wide), BF16),
            pltpu.VMEM((rows, wide), F32),
            pltpu.VMEM((2, tok, wide), BF16),
            dma((3,)), dma((GROUPS,)), dma((GROUPS,)), dma((3,)), dma((3,)), dma((3,)), dma((3,)), dma((2,)), dma,
            dma, dma, dma((PIECES, 2)), dma((PIECES, 2)),
            dma((GROUPS,)), dma((GROUPS,)), dma((GROUPS,)), dma((GROUPS,)),
            dma((GROUPS,)), dma((GROUPS,)), dma((2,)), dma,
        ],
        compiler_params=pltpu.CompilerParams(
            collective_id=0, has_side_effects=True, vmem_limit_bytes=60 * 1024 * 1024
        ),
    )(activations[0], norm_gain, conv_kernels[0], out_gain)
    return handed[None]


def solution(mesh):
    placed = (P("pipe", "seq", None), P("pipe", None), P("pipe", None, None, None), P("pipe", None))
    return jax.shard_map(
        body, mesh=mesh, in_specs=placed, out_specs=P("pipe", "seq", None), check_vma=False
    )
```

```python
import functools

import jax
import jax.numpy as jnp
from jax import lax
from jax.experimental import pallas as pl
from jax.experimental.pallas import tpu as pltpu
from jax.sharding import PartitionSpec as P

DH = 128
HALO = 16
GROUP_HEADS = (4, 4)
OWNER = (0, 1)
FIRST = 1
TILE = 64
SECOND = 3
GROUPS = len(GROUP_HEADS)
RELAY = True
PIECES = 8
EARLY = 2
PAIR = 2
ROW = 8
MESH = pl.DeviceIdType.MESH
F32 = jnp.float32
BF16 = jnp.bfloat16


def lanes(start, size):
    return pl.ds(pl.multiple_of(start, DH), size)


def kernel(
    n_pipe, n_chip, n_y, tok, heads,
    act, ngain, conv, ogain, out,
    own, sx, sf, column, pconv, pngain, pogain, snb, sk, sv, hsend, chalo, rhalo,
    tsend, trecv, rsend, rrecv, psend, pbuf, rx, rf, rnb, rq, rk, rv, within, res,
    relay, load_sem, xs, xr, fs, fr, ps, pr, hs, hr, gs, gr, zs, zr,
    ts, tr, es, er, qs, qr, os_sem, or_sem,
):
    wide = heads * DH
    rows = 2 * tok
    firsts = [sum(GROUP_HEADS[:group]) for group in range(GROUPS)]
    rows_each = DH // n_y
    n_x = n_chip // n_y
    pipe = lax.axis_index("pipe")
    seq = lax.axis_index("seq")
    core = seq % 2
    chip = seq // 2
    x_at = chip // n_y
    y_at = chip % n_y
    ahead = (pipe + 1) % n_pipe
    behind = (pipe + n_pipe - 1) % n_pipe
    peer = seq + 1 - 2 * core
    next_chip = (chip + 1) % n_chip
    last_chip = (chip + n_chip - 1) % n_chip
    y_steps = sorted(range(1, n_y), key=lambda k: -min(k, n_y - k))
    far = n_y // 2 if RELAY and n_y >= 4 else 0
    near_steps = [step for step in y_steps if step != far]
    x_steps = sorted(range(1, n_x), key=lambda k: -min(k, n_x - k))

    def on_row(step):
        return (y_at + step) % n_y

    def row_seq(y):
        return 2 * (x_at * n_y + y) + core

    def column_seq(x):
        return 2 * (x * n_y + y_at) + core

    def remote(src, dst, send, recv, to_pipe, to_seq):
        return pltpu.make_async_remote_copy(
            src_ref=src, dst_ref=dst, send_sem=send, recv_sem=recv,
            device_id=(to_pipe, to_seq), device_id_type=MESH,
        )

    def greet(to_pipe, to_seq):
        pl.semaphore_signal(barrier, inc=1, device_id=(to_pipe, to_seq), device_id_type=MESH)

    pending = []

    def finished():
        for wait in pending:
            wait()

    barrier = pltpu.get_barrier_semaphore()
    greet(pipe, peer)
    for which in range(2):
        greet(behind, 2 * chip + which)
    greet(pipe, 2 * last_chip + 1)
    for step in near_steps:
        greet(pipe, row_seq(on_row(step)))
    if 1 in OWNER:
        for step in y_steps:
            greet(behind, row_seq(on_row(step)))
    for step in x_steps:
        greet(pipe, column_seq((x_at + step) % n_x))

    @pl.when(chip == 0)
    def _():
        chalo[...] = jnp.zeros(chalo.shape, BF16)
        rhalo[...] = jnp.zeros(rhalo.shape, BF16)

    half = lanes(core * wide, wide)
    loads = [
        pltpu.make_async_copy(act, own, load_sem.at[0]),
        pltpu.make_async_copy(conv.at[:, :, half], pconv.at[0], load_sem.at[1]),
        pltpu.make_async_copy(ngain, pngain.at[0], load_sem.at[2]),
    ]
    for load in loads:
        load.start()
    for load in loads:
        load.wait()

    squares = jnp.zeros((tok, DH), F32)
    for piece in range(2 * wide // DH):
        values = own[:, piece * DH : (piece + 1) * DH].astype(F32)
        squares = squares + values * values
    mean = jnp.sum(squares, axis=-1, keepdims=True) * (1.0 / (2 * wide))
    factor = jnp.broadcast_to(lax.rsqrt(mean + 1e-06), (tok, DH))
    column[0] = factor
    sf[0] = factor.T[:8]

    def halo_rows(head, carry):
        cols = lanes(head * DH, DH)
        hsend[:, cols] = (
            own[tok - HALO :, cols].astype(F32) * column[0, tok - HALO :, :] * pngain[0, :, cols]
        ).astype(BF16)
        return carry

    lax.fori_loop(0, 2 * heads, halo_rows, 0, unroll=True)

    def positive(x):
        return jnp.where(x > 0.0, x + 1.0, jnp.exp(jnp.minimum(x, 0.0)))

    def convolved(ref, start, count, which, j, cols):
        total = pconv[which, j, 0:1, cols] * ref[pl.ds(HALO + start, count), cols]
        for i in range(1, 4):
            total = total + pconv[which, j, i : i + 1, cols] * ref[
                pl.ds(HALO + start - i, count), cols
            ]
        return total

    def keys_values(slot, start, count, head):
        cols = lanes(head * DH, DH)
        ref = snb.at[slot]
        where = pl.ds(slot * tok + start, count)
        sk[where, cols] = positive(convolved(ref, start, count, 0, 1, cols)).astype(BF16)
        sv[where, cols] = convolved(ref, start, count, 0, 2, cols).astype(BF16)

    def state_rows(slot, first, last):
        def one(head, carry):
            cols = lanes(head * DH, DH)
            raw = own[:, lanes(core * wide + head * DH, DH)] if slot == 0 else sx[:, cols]
            normed = (
                raw.astype(F32) * column[slot] * pngain[0, :, lanes(core * wide + head * DH, DH)]
            ).astype(BF16)
            snb[slot, HALO:, cols] = normed.astype(F32)
            keys_values(slot, HALO, tok - HALO, head)
            return carry

        lax.fori_loop(first, last, one, 0, unroll=True)

    pl.semaphore_wait(barrier, 3 + len(near_steps) + (1 in OWNER) * len(y_steps) + len(x_steps) + 2 * core)
    if far:
        pl.semaphore_signal(
            relay, inc=1, device_id=(pipe, row_seq(on_row(n_y - 1))), device_id_type=MESH
        )

    x_copies = [
        remote(
            act.at[:, lanes((1 - core) * wide + chunk * (wide // 2), wide // 2)],
            sx.at[:, pl.ds(chunk * (wide // 2), wide // 2)],
            xs.at[chunk], xr.at[chunk], pipe, peer,
        )
        for chunk in range(2)
    ]
    f_copies = [remote(sf.at[0], sf.at[1], fs.at[0], fr.at[0], pipe, peer)]
    for which in range(2):
        f_copies.append(
            remote(sf.at[0], rf.at[core], fs.at[1 + which], fr.at[1 + core], ahead, 2 * chip + which)
        )
    h_copies = [
        remote(
            hsend.at[:, pl.ds(which * wide, wide)], chalo,
            hs.at[which], hr, pipe, 2 * next_chip + which,
        )
        for which in range(2)
    ]
    p_copies = [
        remote(conv.at[:, :, half], pconv.at[1], ps.at[0], pr.at[0], ahead, seq),
        remote(ngain, pngain.at[1], ps.at[1], pr.at[1], ahead, seq),
        remote(ogain, pogain, ps.at[2], pr.at[2], ahead, seq),
    ]

    pwide = wide // PIECES

    def raw_copy(piece, which):
        return remote(
            act.at[:, pl.ds(which * wide + piece * pwide, pwide)],
            rx.at[core, :, pl.ds(piece * pwide, pwide)],
            zs.at[piece, which], zr.at[piece, core], ahead, 2 * chip + which,
        )

    def send_raw(first, last):
        for piece in range(first, last):
            for which in range(2):
                copy = raw_copy(piece, which)
                copy.start()
                pending.append(copy.wait_send)

    sends_halo = jnp.logical_and(core == 1, next_chip != 0)

    @pl.when(sends_halo)
    def _():
        for copy in h_copies:
            copy.start()

    f_copies[0].start()
    for copy in x_copies:
        copy.start()
    for copy in f_copies[1:] + p_copies:
        copy.start()
    send_raw(0, EARLY)

    def wait_sent_halo():
        @pl.when(sends_halo)
        def _():
            for copy in h_copies:
                copy.wait_send()

    pending.append(wait_sent_halo)
    pending.extend(copy.wait_send for copy in x_copies)
    pending.append(f_copies[0].wait_send)
    pending.extend(copy.wait_send for copy in f_copies[1:] + p_copies)

    state_rows(0, 0, heads)
    f_copies[0].wait_recv()
    column[1] = jnp.broadcast_to(sf[1, 0:1, :], (tok, tok)).T
    def edges(group):
        cols = pl.ds(firsts[group] * DH, GROUP_HEADS[group] * DH)
        before = chalo[:, cols].astype(F32)
        snb[0, :HALO, cols] = jnp.where(core == 0, before, snb[1, tok:, cols])
        snb[1, :HALO, cols] = jnp.where(core == 0, snb[0, tok:, cols], before)

    def part(group):
        return GROUP_HEADS[group] * rows_each

    def held(group):
        return pl.ds(firsts[group] * rows_each, part(group))

    def slice_of(group, y):
        return pl.ds(pl.multiple_of(firsts[group] * DH + y * part(group), 16), part(group))

    def t_copy(group, y):
        return remote(
            tsend.at[slice_of(group, y)], trecv.at[y_at, held(group)],
            ts.at[group], tr.at[group], (pipe, ahead)[OWNER[group]], row_seq(y),
        )

    def t_all(group):
        count = n_y - 1 + OWNER[group]
        return remote(
            psend.at[pl.ds(0, count), held(group)], trecv.at[pl.ds(0, count), held(group)],
            ts.at[group], tr.at[group], pipe, peer,
        )

    for chunk in range(2):
        x_copies[chunk].wait_recv()
        state_rows(1, chunk * (heads // 2), (chunk + 1) * (heads // 2))
    g_copy = remote(chalo, rhalo, gs, gr, ahead, seq)

    @pl.when(chip != 0)
    def _():
        h_copies[0].wait_recv()
        g_copy.start()

    def wait_sent_on():
        @pl.when(chip != 0)
        def _():
            g_copy.wait_send()

    pending.append(wait_sent_on)
    for group in range(GROUPS):
        edges(group)

        def one(index, carry, group=group):
            head = firsts[group] + index
            cols = lanes(head * DH, DH)
            for slot in range(2):
                keys_values(slot, 0, HALO, head)
            state = lax.dot_general(
                sk[:, cols], sv[:, cols], (((0,), (0,)), ((), ())), preferred_element_type=F32
            )
            tsend[lanes(head * DH, DH), :] = state.astype(BF16)
            return carry

        lax.fori_loop(0, GROUP_HEADS[group], one, 0, unroll=True)
        if OWNER[group] == 1:
            for step in y_steps + [0]:
                t_copy(group, on_row(step)).start()
        else:
            for step in near_steps:
                t_copy(group, on_row(step)).start()
            if far:
                if group == 0:
                    pl.semaphore_wait(relay, 1)
                t_copy(group, on_row(far)).start()
            trecv[y_at, held(group), :] = tsend[slice_of(group, y_at), :]
        pending.append(t_all(group).wait_send)
    send_raw(EARLY, PIECES)

    def arrived_raw(piece):
        for which in range(2):
            remote(
                sx.at[:, pl.ds(0, pwide)], rx.at[which, :, pl.ds(piece * pwide, pwide)],
                xs.at[0], zr.at[piece, which], ahead, seq,
            ).wait_recv()

    def arrived_first():
        for which in range(2):
            remote(sf.at[0], rf.at[which], fs.at[0], fr.at[1 + which], ahead, seq).wait_recv()
        for copy in p_copies:
            copy.wait_recv()

        @pl.when(chip != 0)
        def _():
            g_copy.wait_recv()

    def e_copy(group, x):
        return remote(
            rsend.at[held(group)], rrecv.at[x_at, held(group)],
            es.at[group], er.at[group], pipe, column_seq(x),
        )

    def e_all(group):
        return remote(
            psend.at[pl.ds(0, n_x - 1), held(group)], rrecv.at[pl.ds(0, n_x - 1), held(group)],
            es.at[group], er.at[group], pipe, peer,
        )

    def q_copy(group, y):
        return remote(
            psend.at[y, held(group)], pbuf.at[slice_of(group, y_at)],
            qs.at[group], qr.at[group], (ahead, pipe)[OWNER[group]], row_seq(y),
        )

    def q_all(group):
        count = GROUP_HEADS[group] * DH - OWNER[group] * part(group)
        where = pl.ds(firsts[group] * DH, count)
        return remote(tsend.at[where], pbuf.at[where], qs.at[group], qr.at[group], ahead, seq)

    def totals(group):
        t_all(group).wait_recv()
        total = trecv[0, held(group), :].astype(F32)
        for y in range(1, n_y):
            total = total + trecv[y, held(group), :].astype(F32)
        rsend[held(group), :] = total.astype(BF16)
        for step in x_steps:
            e_copy(group, (x_at + step) % n_x).start()
        rrecv[x_at, held(group), :] = rsend[held(group), :]
        pending.append(e_all(group).wait_send)

    def prefixes(group):
        e_all(group).wait_recv()
        total = jnp.zeros((part(group), DH), F32)
        for x in range(n_x):
            total = total + jnp.where(x < x_at, rrecv[x, held(group), :].astype(F32), 0.0)
        for y in range(n_y):
            psend[y, held(group), :] = total.astype(BF16)
            total = total + trecv[y, held(group), :].astype(F32)
        for step in y_steps + [0] * (1 - OWNER[group]):
            q_copy(group, on_row(step)).start()
        if OWNER[group] == 1:
            pbuf[slice_of(group, y_at), :] = psend[y_at, held(group), :]
        pending.append(q_all(group).wait_send)

    def own_half(head):
        return lanes(core * wide + head * DH, DH)

    def first_of_behind():
        arrived_first()
        for block in range(2):
            column[block] = jnp.broadcast_to(rf[block, 0:1, :], (tok, tok)).T
        rnb[:HALO, :] = rhalo[...].astype(F32)

    def inside(piece):
        arrived_raw(piece)
        tile = TILE
        query_at = lax.broadcasted_iota(jnp.int32, (tok, rows), 0)
        key_at = lax.broadcasted_iota(jnp.int32, (tok, rows), 1)

        def one(index, carry):
            head = piece * (heads // PIECES) + index
            cols = lanes(head * DH, DH)
            for block in range(2):
                normed = (
                    rx[block, :, cols].astype(F32) * column[block] * pngain[1, :, own_half(head)]
                ).astype(BF16)
                rnb[pl.ds(HALO + block * tok, tok), cols] = normed.astype(F32)
            for start in range(0, rows, tile):
                where = pl.ds(start, tile)
                rq[where, cols] = positive(convolved(rnb, start, tile, 1, 0, cols)).astype(BF16)
                rk[where, cols] = positive(convolved(rnb, start, tile, 1, 1, cols)).astype(BF16)
                rv[where, cols] = convolved(rnb, start, tile, 1, 2, cols).astype(BF16)
            for block in range(2):
                here, until = pl.ds(block * tok, tok), (block + 1) * tok
                scores = lax.dot_general(
                    rq[here, cols], rk[:until, cols], (((1,), (1,)), ((), ())),
                    preferred_element_type=F32,
                )
                causal = key_at[:, :until] <= query_at[:, :until] + block * tok
                weights = jnp.where(causal, scores, 0.0).astype(BF16)
                within[here, cols] = jnp.dot(
                    weights, rv[:until, cols], preferred_element_type=F32
                )
            return carry

        lax.fori_loop(0, heads // PIECES, one, 0, unroll=True)

    def o_copy(first, count):
        cols = lanes(core * wide + first * DH, count * DH)
        return remote(
            res.at[1 - core, :, pl.ds(first * DH, count * DH)], out.at[:, cols],
            os_sem.at[0], or_sem, pipe, peer,
        )

    def keep_copy(first, count):
        cols = lanes(core * wide + first * DH, count * DH)
        return pltpu.make_async_copy(
            res.at[core, :, pl.ds(first * DH, count * DH)], out.at[:, cols], os_sem.at[1]
        )

    def finish(group):
        q_all(group).wait_recv()
        average = jnp.full((DH, DH), 1.0 / DH, BF16)

        for pair in range(GROUP_HEADS[group] // PAIR):
            first = firsts[group] + PAIR * pair
            mixed = []
            for head in range(first, first + PAIR):
                cols = lanes(head * DH, DH)
                mixed.append(
                    within[:, cols]
                    + jnp.dot(rq[:, cols], pbuf[cols, :], preferred_element_type=F32)
                )
            squares = [
                jnp.dot((m * m).astype(BF16), average, preferred_element_type=F32) for m in mixed
            ]
            for k in range(PAIR):
                cols = lanes((first + k) * DH, DH)
                scaled = (
                    mixed[k] * lax.rsqrt(squares[k] + 1e-06) * pogain[:, own_half(first + k)]
                )
                for block in range(2):
                    res[block, :, cols] = (
                        rx[block, :, cols].astype(F32) + scaled[block * tok : (block + 1) * tok]
                    ).astype(BF16)
            o_copy(first, PAIR).start()
            keep_copy(first, PAIR).start()

    if OWNER[-1] == 0:
        for group in range(GROUPS):
            totals(group)
        for group in range(GROUPS):
            prefixes(group)
        first_of_behind()
        for piece in range(PIECES):
            inside(piece)
    else:
        totals(0)
        prefixes(0)
        first_of_behind()
        for piece in range(FIRST):
            inside(piece)
        totals(1)
        for piece in range(FIRST, SECOND):
            inside(piece)
        prefixes(1)
        for piece in range(SECOND, PIECES):
            inside(piece)
    for group in range(GROUPS):
        finish(group)

    everything = remote(
        res.at[1 - core], out.at[:, lanes((1 - core) * wide, wide)], os_sem.at[0], or_sem, pipe, peer
    )
    everything.wait_send()
    everything.wait_recv()
    pltpu.make_async_copy(res.at[core], out.at[:, half], os_sem.at[1]).wait()
    finished()


def body(activations, norm_gain, conv_kernels, out_gain):
    n_pipe = lax.axis_size("pipe")
    n_chip = lax.axis_size("seq") // 2
    n_y = min(ROW, n_chip)
    n_x = n_chip // n_y
    _, tok, width = activations.shape
    wide = width // 2
    heads = wide // DH
    held = wide // n_y
    rows = 2 * tok
    dma = pltpu.SemaphoreType.DMA
    handed = pl.pallas_call(
        functools.partial(kernel, n_pipe, n_chip, n_y, tok, heads),
        out_shape=pltpu.VMEM((tok, width), BF16),
        in_specs=[pl.BlockSpec(memory_space=pltpu.HBM)] * 4,
        out_specs=pl.BlockSpec(memory_space=pl.ANY),
        scratch_shapes=[
            pltpu.VMEM((tok, width), BF16),
            pltpu.VMEM((tok, wide), BF16),
            pltpu.VMEM((2, 8, tok), F32),
            pltpu.VMEM((2, tok, DH), F32),
            pltpu.VMEM((2, 3, 4, wide), F32),
            pltpu.VMEM((2, 1, width), F32),
            pltpu.VMEM((1, width), F32),
            pltpu.VMEM((2, HALO + tok, wide), F32),
            pltpu.VMEM((rows, wide), BF16),
            pltpu.VMEM((rows, wide), BF16),
            pltpu.VMEM((HALO, width), BF16),
            pltpu.VMEM((HALO, wide), BF16),
            pltpu.VMEM((HALO, wide), BF16),
            pltpu.VMEM((wide, DH), BF16),
            pltpu.VMEM((n_y, held, DH), BF16),
            pltpu.VMEM((held, DH), BF16),
            pltpu.VMEM((n_x, held, DH), BF16),
            pltpu.VMEM((n_y, held, DH), BF16),
            pltpu.VMEM((wide, DH), BF16),
            pltpu.VMEM((2, tok, wide), BF16),
            pltpu.VMEM((2, 8, tok), F32),
            pltpu.VMEM((HALO + rows, wide), F32),
            pltpu.VMEM((rows, wide), BF16),
            pltpu.VMEM((rows, wide), BF16),
            pltpu.VMEM((rows, wide), BF16),
            pltpu.VMEM((rows, wide), F32),
            pltpu.VMEM((2, tok, wide), BF16),
            pltpu.SemaphoreType.REGULAR, dma((3,)), dma((2,)), dma((2,)), dma((3,)), dma((3,)), dma((3,)), dma((3,)), dma((2,)), dma,
            dma, dma, dma((PIECES, 2)), dma((PIECES, 2)),
            dma((GROUPS,)), dma((GROUPS,)), dma((GROUPS,)), dma((GROUPS,)),
            dma((GROUPS,)), dma((GROUPS,)), dma((2,)), dma,
        ],
        compiler_params=pltpu.CompilerParams(
            collective_id=0, has_side_effects=True, vmem_limit_bytes=60 * 1024 * 1024
        ),
    )(activations[0], norm_gain, conv_kernels[0], out_gain)
    return handed[None]


def solution(mesh):
    placed = (P("pipe", "seq", None), P("pipe", None), P("pipe", None, None, None), P("pipe", None))
    return jax.shard_map(
        body, mesh=mesh, in_specs=placed, out_specs=P("pipe", "seq", None), check_vma=False
    )
```

```python
import functools

import jax
import jax.numpy as jnp
from jax import lax
from jax.experimental import pallas as pl
from jax.experimental.pallas import tpu as pltpu
from jax.sharding import PartitionSpec as P

DH = 128
HALO = 16
GROUP_HEADS = (4, 4)
OWNER = (0, 1)
FIRST = 1
TILE = 64
SECOND = 3
GROUPS = len(GROUP_HEADS)
RELAY = False
PIECES = 8
EARLY = 2
PAIR = 2
ROW = 8
MESH = pl.DeviceIdType.MESH
F32 = jnp.float32
BF16 = jnp.bfloat16


def lanes(start, size):
    return pl.ds(pl.multiple_of(start, DH), size)


def kernel(
    n_pipe, n_chip, n_y, tok, heads,
    act, ngain, conv, ogain, out,
    own, sx, sf, column, pconv, pngain, pogain, snb, sk, sv, hsend, chalo, rhalo,
    tsend, trecv, rsend, rrecv, psend, pbuf, rx, rf, rnb, rq, rk, rv, within, res,
    relay, load_sem, xs, xr, fs, fr, ps, pr, hs, hr, gs, gr, zs, zr,
    ts, tr, es, er, qs, qr, os_sem, or_sem,
):
    wide = heads * DH
    rows = 2 * tok
    firsts = [sum(GROUP_HEADS[:group]) for group in range(GROUPS)]
    rows_each = DH // n_y
    n_x = n_chip // n_y
    pipe = lax.axis_index("pipe")
    seq = lax.axis_index("seq")
    core = seq % 2
    chip = seq // 2
    x_at = chip // n_y
    y_at = chip % n_y
    ahead = (pipe + 1) % n_pipe
    behind = (pipe + n_pipe - 1) % n_pipe
    peer = seq + 1 - 2 * core
    next_chip = (chip + 1) % n_chip
    last_chip = (chip + n_chip - 1) % n_chip
    y_steps = sorted(range(1, n_y), key=lambda k: -min(k, n_y - k))
    far = n_y // 2 if RELAY and n_y >= 4 else 0
    near_steps = [step for step in y_steps if step != far]
    x_steps = sorted(range(1, n_x), key=lambda k: -min(k, n_x - k))

    def on_row(step):
        return (y_at + step) % n_y

    def row_seq(y):
        return 2 * (x_at * n_y + y) + core

    def column_seq(x):
        return 2 * (x * n_y + y_at) + core

    def remote(src, dst, send, recv, to_pipe, to_seq):
        return pltpu.make_async_remote_copy(
            src_ref=src, dst_ref=dst, send_sem=send, recv_sem=recv,
            device_id=(to_pipe, to_seq), device_id_type=MESH,
        )

    def greet(to_pipe, to_seq):
        pl.semaphore_signal(barrier, inc=1, device_id=(to_pipe, to_seq), device_id_type=MESH)

    pending = []

    def finished():
        for wait in pending:
            wait()

    barrier = pltpu.get_barrier_semaphore()
    greet(pipe, peer)
    for which in range(2):
        greet(behind, 2 * chip + which)
    greet(pipe, 2 * last_chip + 1)
    for step in near_steps:
        greet(pipe, row_seq(on_row(step)))
    if 1 in OWNER:
        for step in y_steps:
            greet(behind, row_seq(on_row(step)))
    for step in x_steps:
        greet(pipe, column_seq((x_at + step) % n_x))

    @pl.when(chip == 0)
    def _():
        chalo[...] = jnp.zeros(chalo.shape, BF16)
        rhalo[...] = jnp.zeros(rhalo.shape, BF16)

    half = lanes(core * wide, wide)
    loads = [
        pltpu.make_async_copy(act, own, load_sem.at[0]),
        pltpu.make_async_copy(conv.at[:, :, half], pconv.at[0], load_sem.at[1]),
        pltpu.make_async_copy(ngain, pngain.at[0], load_sem.at[2]),
    ]
    for load in loads:
        load.start()
    for load in loads:
        load.wait()

    squares = jnp.zeros((tok, DH), F32)
    for piece in range(2 * wide // DH):
        values = own[:, piece * DH : (piece + 1) * DH].astype(F32)
        squares = squares + values * values
    mean = jnp.sum(squares, axis=-1, keepdims=True) * (1.0 / (2 * wide))
    factor = jnp.broadcast_to(lax.rsqrt(mean + 1e-06), (tok, DH))
    column[0] = factor
    sf[0] = factor.T[:8]

    def halo_rows(head, carry):
        cols = lanes(head * DH, DH)
        hsend[:, cols] = (
            own[tok - HALO :, cols].astype(F32) * column[0, tok - HALO :, :] * pngain[0, :, cols]
        ).astype(BF16)
        return carry

    lax.fori_loop(0, 2 * heads, halo_rows, 0, unroll=True)

    def positive(x):
        return jnp.where(x > 0.0, x + 1.0, jnp.exp(jnp.minimum(x, 0.0)))

    def convolved(ref, start, count, which, j, cols):
        total = pconv[which, j, 0:1, cols] * ref[pl.ds(HALO + start, count), cols]
        for i in range(1, 4):
            total = total + pconv[which, j, i : i + 1, cols] * ref[
                pl.ds(HALO + start - i, count), cols
            ]
        return total

    def keys_values(slot, start, count, head):
        cols = lanes(head * DH, DH)
        ref = snb.at[slot]
        where = pl.ds(slot * tok + start, count)
        sk[where, cols] = positive(convolved(ref, start, count, 0, 1, cols)).astype(BF16)
        sv[where, cols] = convolved(ref, start, count, 0, 2, cols).astype(BF16)

    def state_rows(slot, first, last):
        def one(head, carry):
            cols = lanes(head * DH, DH)
            raw = own[:, lanes(core * wide + head * DH, DH)] if slot == 0 else sx[:, cols]
            normed = (
                raw.astype(F32) * column[slot] * pngain[0, :, lanes(core * wide + head * DH, DH)]
            ).astype(BF16)
            snb[slot, HALO:, cols] = normed.astype(F32)
            keys_values(slot, HALO, tok - HALO, head)
            return carry

        lax.fori_loop(first, last, one, 0, unroll=True)

    pl.semaphore_wait(barrier, 3 + len(near_steps) + (1 in OWNER) * len(y_steps) + len(x_steps) + 2 * core)
    if far:
        pl.semaphore_signal(
            relay, inc=1, device_id=(pipe, row_seq(on_row(n_y - 1))), device_id_type=MESH
        )

    x_copies = [
        remote(
            act.at[:, lanes((1 - core) * wide + chunk * (wide // 2), wide // 2)],
            sx.at[:, pl.ds(chunk * (wide // 2), wide // 2)],
            xs.at[chunk], xr.at[chunk], pipe, peer,
        )
        for chunk in range(2)
    ]
    f_copies = [remote(sf.at[0], sf.at[1], fs.at[0], fr.at[0], pipe, peer)]
    for which in range(2):
        f_copies.append(
            remote(sf.at[0], rf.at[core], fs.at[1 + which], fr.at[1 + core], ahead, 2 * chip + which)
        )
    h_copies = [
        remote(
            hsend.at[:, pl.ds(which * wide, wide)], chalo,
            hs.at[which], hr, pipe, 2 * next_chip + which,
        )
        for which in range(2)
    ]
    p_copies = [
        remote(conv.at[:, :, half], pconv.at[1], ps.at[0], pr.at[0], ahead, seq),
        remote(ngain.at[:, half], pngain.at[1, :, half], ps.at[1], pr.at[1], ahead, seq),
        remote(ogain.at[:, half], pogain.at[:, half], ps.at[2], pr.at[2], ahead, seq),
    ]

    pwide = wide // PIECES

    def raw_copy(piece, which):
        return remote(
            act.at[:, pl.ds(which * wide + piece * pwide, pwide)],
            rx.at[core, :, pl.ds(piece * pwide, pwide)],
            zs.at[piece, which], zr.at[piece, core], ahead, 2 * chip + which,
        )

    def send_raw(first, last):
        for piece in range(first, last):
            for which in range(2):
                copy = raw_copy(piece, which)
                copy.start()
                pending.append(copy.wait_send)

    sends_halo = jnp.logical_and(core == 1, next_chip != 0)

    @pl.when(sends_halo)
    def _():
        for copy in h_copies:
            copy.start()

    f_copies[0].start()
    for copy in x_copies:
        copy.start()
    for copy in f_copies[1:] + p_copies:
        copy.start()
    send_raw(0, EARLY)

    def wait_sent_halo():
        @pl.when(sends_halo)
        def _():
            for copy in h_copies:
                copy.wait_send()

    pending.append(wait_sent_halo)
    pending.extend(copy.wait_send for copy in x_copies)
    pending.append(f_copies[0].wait_send)
    pending.extend(copy.wait_send for copy in f_copies[1:] + p_copies)

    state_rows(0, 0, heads)
    f_copies[0].wait_recv()
    column[1] = jnp.broadcast_to(sf[1, 0:1, :], (tok, tok)).T
    def edges(group):
        cols = pl.ds(firsts[group] * DH, GROUP_HEADS[group] * DH)
        before = chalo[:, cols].astype(F32)
        snb[0, :HALO, cols] = jnp.where(core == 0, before, snb[1, tok:, cols])
        snb[1, :HALO, cols] = jnp.where(core == 0, snb[0, tok:, cols], before)

    def part(group):
        return GROUP_HEADS[group] * rows_each

    def held(group):
        return pl.ds(firsts[group] * rows_each, part(group))

    def slice_of(group, y):
        return pl.ds(pl.multiple_of(firsts[group] * DH + y * part(group), 16), part(group))

    def t_copy(group, y):
        return remote(
            tsend.at[slice_of(group, y)], trecv.at[y_at, held(group)],
            ts.at[group], tr.at[group], (pipe, ahead)[OWNER[group]], row_seq(y),
        )

    def t_all(group):
        count = n_y - 1 + OWNER[group]
        return remote(
            psend.at[pl.ds(0, count), held(group)], trecv.at[pl.ds(0, count), held(group)],
            ts.at[group], tr.at[group], pipe, peer,
        )

    for chunk in range(2):
        x_copies[chunk].wait_recv()
        state_rows(1, chunk * (heads // 2), (chunk + 1) * (heads // 2))
    g_copy = remote(chalo, rhalo, gs, gr, ahead, seq)

    @pl.when(chip != 0)
    def _():
        h_copies[0].wait_recv()
        g_copy.start()

    def wait_sent_on():
        @pl.when(chip != 0)
        def _():
            g_copy.wait_send()

    pending.append(wait_sent_on)
    for group in range(GROUPS):
        edges(group)

        def one(index, carry, group=group):
            head = firsts[group] + index
            cols = lanes(head * DH, DH)
            for slot in range(2):
                keys_values(slot, 0, HALO, head)
            state = lax.dot_general(
                sk[:, cols], sv[:, cols], (((0,), (0,)), ((), ())), preferred_element_type=F32
            )
            tsend[lanes(head * DH, DH), :] = state.astype(BF16)
            return carry

        lax.fori_loop(0, GROUP_HEADS[group], one, 0, unroll=True)
        if OWNER[group] == 1:
            for step in y_steps + [0]:
                t_copy(group, on_row(step)).start()
        else:
            for step in near_steps:
                t_copy(group, on_row(step)).start()
            if far:
                if group == 0:
                    pl.semaphore_wait(relay, 1)
                t_copy(group, on_row(far)).start()
            trecv[y_at, held(group), :] = tsend[slice_of(group, y_at), :]
        pending.append(t_all(group).wait_send)
    send_raw(EARLY, PIECES)

    def arrived_raw(piece):
        for which in range(2):
            remote(
                sx.at[:, pl.ds(0, pwide)], rx.at[which, :, pl.ds(piece * pwide, pwide)],
                xs.at[0], zr.at[piece, which], ahead, seq,
            ).wait_recv()

    def arrived_first():
        for which in range(2):
            remote(sf.at[0], rf.at[which], fs.at[0], fr.at[1 + which], ahead, seq).wait_recv()
        for copy in p_copies:
            copy.wait_recv()

        @pl.when(chip != 0)
        def _():
            g_copy.wait_recv()

    def e_copy(group, x):
        return remote(
            rsend.at[held(group)], rrecv.at[x_at, held(group)],
            es.at[group], er.at[group], pipe, column_seq(x),
        )

    def e_all(group):
        return remote(
            psend.at[pl.ds(0, n_x - 1), held(group)], rrecv.at[pl.ds(0, n_x - 1), held(group)],
            es.at[group], er.at[group], pipe, peer,
        )

    def q_copy(group, y):
        return remote(
            psend.at[y, held(group)], pbuf.at[slice_of(group, y_at)],
            qs.at[group], qr.at[group], (ahead, pipe)[OWNER[group]], row_seq(y),
        )

    def q_all(group):
        count = GROUP_HEADS[group] * DH - OWNER[group] * part(group)
        where = pl.ds(firsts[group] * DH, count)
        return remote(tsend.at[where], pbuf.at[where], qs.at[group], qr.at[group], ahead, seq)

    def totals(group):
        t_all(group).wait_recv()
        total = trecv[0, held(group), :].astype(F32)
        for y in range(1, n_y):
            total = total + trecv[y, held(group), :].astype(F32)
        rsend[held(group), :] = total.astype(BF16)
        for step in x_steps:
            e_copy(group, (x_at + step) % n_x).start()
        rrecv[x_at, held(group), :] = rsend[held(group), :]
        pending.append(e_all(group).wait_send)

    def prefixes(group):
        e_all(group).wait_recv()
        total = jnp.zeros((part(group), DH), F32)
        for x in range(n_x):
            total = total + jnp.where(x < x_at, rrecv[x, held(group), :].astype(F32), 0.0)
        for y in range(n_y):
            psend[y, held(group), :] = total.astype(BF16)
            total = total + trecv[y, held(group), :].astype(F32)
        for step in y_steps + [0] * (1 - OWNER[group]):
            q_copy(group, on_row(step)).start()
        if OWNER[group] == 1:
            pbuf[slice_of(group, y_at), :] = psend[y_at, held(group), :]
        pending.append(q_all(group).wait_send)

    def own_half(head):
        return lanes(core * wide + head * DH, DH)

    def first_of_behind():
        arrived_first()
        for block in range(2):
            column[block] = jnp.broadcast_to(rf[block, 0:1, :], (tok, tok)).T
        rnb[:HALO, :] = rhalo[...].astype(F32)

    def inside(piece):
        arrived_raw(piece)
        tile = TILE
        query_at = lax.broadcasted_iota(jnp.int32, (tok, rows), 0)
        key_at = lax.broadcasted_iota(jnp.int32, (tok, rows), 1)

        def one(index, carry):
            head = piece * (heads // PIECES) + index
            cols = lanes(head * DH, DH)
            for block in range(2):
                normed = (
                    rx[block, :, cols].astype(F32) * column[block] * pngain[1, :, own_half(head)]
                ).astype(BF16)
                rnb[pl.ds(HALO + block * tok, tok), cols] = normed.astype(F32)
            for start in range(0, rows, tile):
                where = pl.ds(start, tile)
                rq[where, cols] = positive(convolved(rnb, start, tile, 1, 0, cols)).astype(BF16)
                rk[where, cols] = positive(convolved(rnb, start, tile, 1, 1, cols)).astype(BF16)
                rv[where, cols] = convolved(rnb, start, tile, 1, 2, cols).astype(BF16)
            for block in range(2):
                here, until = pl.ds(block * tok, tok), (block + 1) * tok
                scores = lax.dot_general(
                    rq[here, cols], rk[:until, cols], (((1,), (1,)), ((), ())),
                    preferred_element_type=F32,
                )
                causal = key_at[:, :until] <= query_at[:, :until] + block * tok
                weights = jnp.where(causal, scores, 0.0).astype(BF16)
                within[here, cols] = jnp.dot(
                    weights, rv[:until, cols], preferred_element_type=F32
                )
            return carry

        lax.fori_loop(0, heads // PIECES, one, 0, unroll=True)

    def o_copy(first, count):
        cols = lanes(core * wide + first * DH, count * DH)
        return remote(
            res.at[1 - core, :, pl.ds(first * DH, count * DH)], out.at[:, cols],
            os_sem.at[0], or_sem, pipe, peer,
        )

    def keep_copy(first, count):
        cols = lanes(core * wide + first * DH, count * DH)
        return pltpu.make_async_copy(
            res.at[core, :, pl.ds(first * DH, count * DH)], out.at[:, cols], os_sem.at[1]
        )

    def finish(group):
        q_all(group).wait_recv()
        average = jnp.full((DH, DH), 1.0 / DH, BF16)

        for pair in range(GROUP_HEADS[group] // PAIR):
            first = firsts[group] + PAIR * pair
            mixed = []
            for head in range(first, first + PAIR):
                cols = lanes(head * DH, DH)
                mixed.append(
                    within[:, cols]
                    + jnp.dot(rq[:, cols], pbuf[cols, :], preferred_element_type=F32)
                )
            squares = [
                jnp.dot((m * m).astype(BF16), average, preferred_element_type=F32) for m in mixed
            ]
            for k in range(PAIR):
                cols = lanes((first + k) * DH, DH)
                scaled = (
                    mixed[k] * lax.rsqrt(squares[k] + 1e-06) * pogain[:, own_half(first + k)]
                )
                for block in range(2):
                    res[block, :, cols] = (
                        rx[block, :, cols].astype(F32) + scaled[block * tok : (block + 1) * tok]
                    ).astype(BF16)
            o_copy(first, PAIR).start()
            keep_copy(first, PAIR).start()

    if OWNER[-1] == 0:
        for group in range(GROUPS):
            totals(group)
        for group in range(GROUPS):
            prefixes(group)
        first_of_behind()
        for piece in range(PIECES):
            inside(piece)
    else:
        totals(0)
        prefixes(0)
        first_of_behind()
        for piece in range(FIRST):
            inside(piece)
        totals(1)
        for piece in range(FIRST, SECOND):
            inside(piece)
        prefixes(1)
        for piece in range(SECOND, PIECES):
            inside(piece)
    for group in range(GROUPS):
        finish(group)

    everything = remote(
        res.at[1 - core], out.at[:, lanes((1 - core) * wide, wide)], os_sem.at[0], or_sem, pipe, peer
    )
    everything.wait_send()
    everything.wait_recv()
    pltpu.make_async_copy(res.at[core], out.at[:, half], os_sem.at[1]).wait()
    finished()


def body(activations, norm_gain, conv_kernels, out_gain):
    n_pipe = lax.axis_size("pipe")
    n_chip = lax.axis_size("seq") // 2
    n_y = min(ROW, n_chip)
    n_x = n_chip // n_y
    _, tok, width = activations.shape
    wide = width // 2
    heads = wide // DH
    held = wide // n_y
    rows = 2 * tok
    dma = pltpu.SemaphoreType.DMA
    handed = pl.pallas_call(
        functools.partial(kernel, n_pipe, n_chip, n_y, tok, heads),
        out_shape=pltpu.VMEM((tok, width), BF16),
        in_specs=[pl.BlockSpec(memory_space=pltpu.HBM)] * 4,
        out_specs=pl.BlockSpec(memory_space=pl.ANY),
        scratch_shapes=[
            pltpu.VMEM((tok, width), BF16),
            pltpu.VMEM((tok, wide), BF16),
            pltpu.VMEM((2, 8, tok), F32),
            pltpu.VMEM((2, tok, DH), F32),
            pltpu.VMEM((2, 3, 4, wide), F32),
            pltpu.VMEM((2, 1, width), F32),
            pltpu.VMEM((1, width), F32),
            pltpu.VMEM((2, HALO + tok, wide), F32),
            pltpu.VMEM((rows, wide), BF16),
            pltpu.VMEM((rows, wide), BF16),
            pltpu.VMEM((HALO, width), BF16),
            pltpu.VMEM((HALO, wide), BF16),
            pltpu.VMEM((HALO, wide), BF16),
            pltpu.VMEM((wide, DH), BF16),
            pltpu.VMEM((n_y, held, DH), BF16),
            pltpu.VMEM((held, DH), BF16),
            pltpu.VMEM((n_x, held, DH), BF16),
            pltpu.VMEM((n_y, held, DH), BF16),
            pltpu.VMEM((wide, DH), BF16),
            pltpu.VMEM((2, tok, wide), BF16),
            pltpu.VMEM((2, 8, tok), F32),
            pltpu.VMEM((HALO + rows, wide), F32),
            pltpu.VMEM((rows, wide), BF16),
            pltpu.VMEM((rows, wide), BF16),
            pltpu.VMEM((rows, wide), BF16),
            pltpu.VMEM((rows, wide), F32),
            pltpu.VMEM((2, tok, wide), BF16),
            pltpu.SemaphoreType.REGULAR, dma((3,)), dma((2,)), dma((2,)), dma((3,)), dma((3,)), dma((3,)), dma((3,)), dma((2,)), dma,
            dma, dma, dma((PIECES, 2)), dma((PIECES, 2)),
            dma((GROUPS,)), dma((GROUPS,)), dma((GROUPS,)), dma((GROUPS,)),
            dma((GROUPS,)), dma((GROUPS,)), dma((2,)), dma,
        ],
        compiler_params=pltpu.CompilerParams(
            collective_id=0, has_side_effects=True, vmem_limit_bytes=60 * 1024 * 1024
        ),
    )(activations[0], norm_gain, conv_kernels[0], out_gain)
    return handed[None]


def solution(mesh):
    placed = (P("pipe", "seq", None), P("pipe", None), P("pipe", None, None, None), P("pipe", None))
    return jax.shard_map(
        body, mesh=mesh, in_specs=placed, out_specs=P("pipe", "seq", None), check_vma=False
    )
```
